32 devices in a mesh: ctx: 16 (over z, y, core), kv: 2 (over x).
Axes of the slice: x: 2, y: 2, z: 4, core: 2. Of those that a mesh axis runs over, the one named last changes fastest.
Arguments:
- queries: float32 [2, 1024, 16384], P(None, 'ctx', 'kv'), may hold values from -5 to 5
- keys: float32 [2, 1024, 1024], P(None, 'ctx', 'kv'), may hold values from -5 to 5
- values: float32 [2, 1024, 1024], P(None, 'ctx', 'kv'), may hold values from -6 to 6
- query_maps: float32 [128, 128, 128], P('kv'), may hold values from -2.5 to 2.5
- key_maps: float32 [8, 128, 128], P('kv'), may hold values from -2.5 to 2.5
- mix: float32 [128], P('kv'), may hold values from -2 to 2
- window_blocks: int32 [2, 16], P(None, 'ctx'), may hold values from 0 to 255
- starts: int32 [2], replicated, may hold values from 0 to 256, as said below
Outputs:
- attended: float32 [2, 1024, 16384], P(None, ('ctx', 'kv'))
The draws below stay inside these ranges and needn't reach their ends.
Inputs may be any that keep to these rules, and one draw needn't show every extreme that they name: Every start lies between 0 and 256; some sequence starts exactly at 256.
All inputs are finite; a program needn't handle non-finite values.
Results may differ from the reference program's by a relative error of at most 0.0003.
Values sent between devices are 32-bit elements; how exact they have to be, the bound alone decides.
No kernel may reach another device: no remote copies, remote signals or barrier semaphores. Data moves between devices by JAX's collectives and lax.ppermute only.
A program may use at most 128 MiB of HBM per device.

```python
import jax
import jax.numpy as jnp
from jax import lax

QH = 128
KVH = 8
HD = 128
HALF = 128
BLOCK = 64
WBLK = 8
SEQS = 2
LENGTH = 1024
NBLK = 16


def draw_starts(key, part):
    first_key, second_key = jax.random.split(jax.random.fold_in(key, 11), 2)
    drawn = jax.random.randint(first_key, (SEQS,), 0, LENGTH // 4 + 1)
    chosen = jax.random.randint(second_key, (), 0, SEQS)
    index = jnp.arange(SEQS)
    return jnp.where(index == chosen, LENGTH // 4, drawn).astype(jnp.int32)


def plant_layout(key):
    base = jax.random.fold_in(key, 101)
    block_key, offset_key, head_key, sign_key = jax.random.split(base, 4)
    first = NBLK // 4
    count = min(8, NBLK - first)
    seq_keys = jax.random.split(block_key, SEQS)
    blocks = jax.vmap(lambda one_key: jax.random.permutation(one_key, NBLK - first)[:count])(seq_keys) + first
    offsets = jax.random.randint(offset_key, (SEQS, count), 2, BLOCK)
    heads = jax.random.randint(head_key, (SEQS, count), 0, QH)
    signs = (2 * jax.random.randint(sign_key, (SEQS, count, HD), 0, 2) - 1).astype(jnp.float32)
    levels = jnp.array([3.2, 4.2, 5.0], dtype=jnp.float32)
    strengths = levels[jnp.arange(count) % 3]
    positions = (blocks * BLOCK + offsets).astype(jnp.int32)
    return (positions, heads.astype(jnp.int32), signs, strengths)


def base_field(key, width):
    noise_key = jax.random.fold_in(key, 0)
    field = jax.random.normal(noise_key, (SEQS, LENGTH, width), jnp.float32)
    return jnp.clip(field, -4.0, 4.0)


def draw_queries(key, part):
    field = base_field(jax.random.fold_in(key, 7), QH * HD)
    positions, heads, signs, strengths = plant_layout(key)
    columns = heads[:, :, None] * HD + jnp.arange(HD, dtype=jnp.int32)[None, None, :]
    seq_index = jnp.arange(SEQS, dtype=jnp.int32)[:, None, None]
    planted = strengths[None, :, None] * signs
    return field.at[seq_index, positions[:, :, None], columns].set(planted)


def draw_keys(key, part):
    field = base_field(jax.random.fold_in(key, 9), KVH * HD)
    positions, heads, signs, strengths = plant_layout(key)
    kv_heads = heads // (QH // KVH)
    columns = kv_heads[:, :, None] * HD + jnp.arange(HD, dtype=jnp.int32)[None, None, :]
    seq_index = jnp.arange(SEQS, dtype=jnp.int32)[:, None, None]
    near_level = strengths[None, :, None] * signs
    lower = strengths - 2.0 / (strengths * HD ** 0.5)
    second_level = lower[None, :, None] * signs
    field = field.at[seq_index, positions[:, :, None] - 1, columns].set(near_level)
    return field.at[seq_index, positions[:, :, None] - 2, columns].set(second_level)


def set_ends(values, key, smallest, largest):
    spot = [jax.random.randint(jax.random.fold_in(key, axis), (), 0, length) for axis, length in enumerate(values.shape)]
    main_axis = values.shape.index(max(values.shape))
    neighbour = spot[:main_axis] + [(spot[main_axis] + 1) % values.shape[main_axis]] + spot[main_axis + 1:]
    return values.at[tuple(spot)].set(smallest).at[tuple(neighbour)].set(largest)


def block_scale(rng, extent, pieces, least, top_value):
    loudness = 1.0
    for dim, blocks in pieces:
        draws = jax.random.uniform(jax.random.fold_in(jax.random.fold_in(rng, 6), dim), (blocks,), jnp.float32, least / len(pieces), top_value / len(pieces))
        loudness = loudness * jnp.repeat(jnp.exp(draws), extent[dim] // blocks).reshape((-1,) + (1,) * (len(extent) - 1 - dim))
    return loudness


def scatter_about(rng, dims, scale, reach, pieces=(), held_as=jnp.bfloat16):
    factor_of = block_scale(rng, dims, pieces, -0.22, 0.18) if pieces else 1.0
    values = jax.random.normal(rng, dims, jnp.float32) * scale * factor_of
    return jnp.minimum(jnp.maximum(values, -reach), reach).astype(held_as)


def setup_inputs(seed: int = 0) -> dict:
    seeds = jax.random.split(jax.random.key(seed), 9)
    queries = draw_queries(jax.random.fold_in(seeds[8], 71), 0)
    keys = draw_keys(jax.random.fold_in(seeds[8], 71), 0)
    values = scatter_about(seeds[2], (SEQS, LENGTH, KVH * HD), 1.0, 6.0, ((1, 16), (2, 2)), jnp.float32)
    query_maps = scatter_about(seeds[3], (QH, HD, HALF), 0.25, 2.5, ((0, 2),), jnp.float32)
    key_maps = scatter_about(seeds[4], (KVH, HD, HALF), 0.25, 2.5, ((0, 2),), jnp.float32)
    mix = jnp.clip(jax.random.uniform(seeds[5], (QH,), jnp.float32, -2.0, 2.0) * block_scale(seeds[5], (QH,), ((0, 2),), -0.4, 0.0), -2.0, 2.0)
    window_blocks = set_ends(jax.random.randint(seeds[6], (SEQS, NBLK), 0, 256), jax.random.fold_in(seeds[6], 1), 0, 255).astype(jnp.int32)
    starts = draw_starts(jax.random.fold_in(seeds[8], 71), 0)
    return dict(queries=queries, keys=keys, values=values, query_maps=query_maps, key_maps=key_maps, mix=mix, window_blocks=window_blocks, starts=starts)


highest = lax.Precision.HIGHEST


def featurize(inputs, feature_maps):
    logits = jnp.einsum("...hd,hdf->...hf", inputs, feature_maps, precision=highest)
    upper_exp = jnp.exp(logits)
    lower_exp = jnp.exp(-logits)
    return jnp.concatenate([upper_exp / jnp.sum(upper_exp, axis=-1, keepdims=True), lower_exp / jnp.sum(lower_exp, axis=-1, keepdims=True)], axis=-1)


def window_mask(pattern_bits, key_live):
    window_len = (WBLK + 1) * BLOCK
    row_ids = jnp.arange(BLOCK, dtype=jnp.int32)[:, None]
    col_ids = jnp.arange(window_len, dtype=jnp.int32)[None, :]
    key_block = col_ids // BLOCK
    distance = WBLK - key_block
    divisor = jnp.power(2, jnp.maximum(distance - 1, 0)).astype(jnp.int32)
    picked = ((pattern_bits[:, :, None] // divisor) % 2) == 1
    causal = (col_ids - WBLK * BLOCK) <= row_ids
    allowed = jnp.where(key_block == WBLK, causal, picked)
    return allowed & key_live[:, None, :]


def attend_block(query_heads, key_rows, value_rows, allowed, rows_live, features_q, state_now, norm_now, weight):
    scores = jnp.einsum("sbkgd,swkd->skgbw", query_heads, key_rows, precision=highest) * (HD ** -0.5)
    chosen = allowed[:, None, None, :, :]
    row_peak = jnp.max(jnp.where(chosen, scores, -1e30), axis=-1, keepdims=True)
    exp_terms = jnp.where(chosen, jnp.exp(scores - row_peak), 0.0)
    near_sum = jnp.einsum("skgbw,swkd->sbkgd", exp_terms, value_rows, precision=highest)
    near_norm = jnp.einsum("skgbw->sbkg", exp_terms)
    far_sum = jnp.einsum("sbkgf,skfd->sbkgd", features_q, state_now, precision=highest)
    far_norm = jnp.einsum("sbkgf,skf->sbkg", features_q, norm_now, precision=highest)
    numerator = weight[:, :, None] * near_sum + (1.0 - weight[:, :, None]) * far_sum
    denominator = weight * near_norm + (1.0 - weight) * far_norm
    live_rows = rows_live[:, :, None, None]
    safe_den = jnp.where(live_rows, denominator, 1.0)
    attended = jnp.where(live_rows[..., None], numerator / safe_den[..., None], 0.0)
    return attended.reshape(attended.shape[0], attended.shape[1], -1)


def reference(queries, keys, values, query_maps, key_maps, mix, window_blocks, starts):
    seq_count, seq_length, query_width = queries.shape
    block_total = seq_length // BLOCK
    groups = QH // KVH
    features = 2 * HALF
    window_len = (WBLK + 1) * BLOCK
    positions = jnp.arange(seq_length, dtype=jnp.int32)
    live = positions[None, :] >= starts.astype(jnp.int32)[:, None]
    key_heads = keys.reshape(seq_count, seq_length, KVH, HD)
    value_heads = values.reshape(seq_count, seq_length, KVH, HD)
    key_features = jnp.where(live[:, :, None, None], featurize(key_heads, key_maps), 0.0)
    blocked_features = key_features.reshape(seq_count, block_total, BLOCK, KVH, features)
    blocked_values = value_heads.reshape(seq_count, block_total, BLOCK, KVH, HD)
    block_states = jnp.einsum("snbkf,snbkd->snkfd", blocked_features, blocked_values, precision=highest)
    block_norms = jnp.sum(blocked_features, axis=2)
    state_sums = jnp.cumsum(block_states, axis=1)
    norm_sums = jnp.cumsum(block_norms, axis=1)
    lead_blocks = WBLK + 1
    far_states = jnp.concatenate([jnp.zeros_like(state_sums[:, :lead_blocks]), state_sums[:, : block_total - lead_blocks]], axis=1)
    far_norms = jnp.concatenate([jnp.zeros_like(norm_sums[:, :lead_blocks]), norm_sums[:, : block_total - lead_blocks]], axis=1)
    pad_rows = WBLK * BLOCK
    key_padded = jnp.concatenate([jnp.zeros_like(key_heads[:, :pad_rows]), key_heads], axis=1)
    value_padded = jnp.concatenate([jnp.zeros_like(value_heads[:, :pad_rows]), value_heads], axis=1)
    live_padded = jnp.concatenate([jnp.zeros_like(live[:, :pad_rows]), live], axis=1)
    weight = jax.nn.sigmoid(mix).reshape(KVH, groups)

    def one_block(block_index):
        row_start = block_index * BLOCK
        query_rows = lax.dynamic_slice_in_dim(queries, row_start, BLOCK, 1).reshape(seq_count, BLOCK, QH, HD)
        features_q = featurize(query_rows, query_maps).reshape(seq_count, BLOCK, KVH, groups, features)
        key_rows = lax.dynamic_slice_in_dim(key_padded, row_start, window_len, 1)
        value_rows = lax.dynamic_slice_in_dim(value_padded, row_start, window_len, 1)
        key_live = lax.dynamic_slice_in_dim(live_padded, row_start, window_len, 1)
        pattern_bits = lax.dynamic_slice_in_dim(window_blocks, block_index, 1, 1)
        allowed = window_mask(pattern_bits, key_live)
        rows_live = lax.dynamic_slice_in_dim(live, row_start, BLOCK, 1)
        state_now = lax.dynamic_index_in_dim(far_states, block_index, 1, keepdims=False)
        norm_now = lax.dynamic_index_in_dim(far_norms, block_index, 1, keepdims=False)
        return attend_block(query_rows.reshape(seq_count, BLOCK, KVH, groups, HD), key_rows, value_rows, allowed, rows_live, features_q, state_now, norm_now, weight)

    outputs = lax.map(one_block, jnp.arange(block_total, dtype=jnp.int32))
    return jnp.moveaxis(outputs, 0, 1).reshape(seq_count, seq_length, query_width)
```

```python
import functools

import jax
import jax.numpy as jnp
from jax import lax
from jax.experimental import pallas as pl
from jax.experimental.pallas import tpu as pltpu
from jax.sharding import PartitionSpec as P

HD = 128
HALF = 128
FAR_ROWS = 2 * HALF
BLOCK = 64
WBLK = 8
STEP_HEADS = 8
UNIT_HEADS = 4
PAIR = 2 * BLOCK
PAIRS = (WBLK + 2) // 2
LEAST_PAIRS = 2
NEAR = 4
LOG2E = 1.4426950408889634
NEG = -1e30
VMEM_LIMIT = 20 * 1024 * 1024

bf16 = jnp.bfloat16
f32 = jnp.float32


def split2(x):
    hi = x.astype(bf16)
    lo = (x - hi.astype(f32)).astype(bf16)
    return hi, lo


def mm(a, b):
    return lax.dot_general(a, b, (((1,), (0,)), ((), ())), preferred_element_type=f32)


def row_offsets(part, parts):
    rows = BLOCK // parts
    return [lax.rem(part + o, parts) * rows for o in range(1, parts)] + [part * rows]


def head_rows(q_ref, s, head, offsets):
    rows = BLOCK // len(offsets)
    cols = pl.ds(pl.multiple_of(head * HD, HD), HD)
    return jnp.concatenate([q_ref[s, pl.ds(pl.multiple_of(off, 8), rows), cols] for off in offsets], axis=0)


def feature_kernel(parts, first_head, meta, ratio, q_ref, maps_ref, hi_ref, lo_ref):
    seqs = q_ref.shape[0]
    offsets = row_offsets(meta[1], parts)

    def some_heads(i, carry):
        for n in range(STEP_HEADS):
            h = i * STEP_HEADS + n
            head = first_head + h
            x = jnp.concatenate([head_rows(q_ref, s, head, offsets) for s in range(seqs)], axis=0)
            x_hi, x_lo = split2(x)
            w_hi, w_lo = split2(maps_ref[head])
            logits = mm(
                jnp.concatenate([x_hi, x_lo, x_hi], axis=1),
                jnp.concatenate([w_hi, w_hi, w_lo], axis=0),
            )
            for m, raw in enumerate((jnp.exp(logits), jnp.exp(-logits))):
                feats = raw * (ratio[head] / jnp.sum(raw, axis=1, keepdims=True))
                p_hi, p_lo = split2(feats)
                hi_ref[h, :, m * HALF:(m + 1) * HALF] = p_hi
                lo_ref[h, :, m * HALF:(m + 1) * HALF] = p_lo
        return carry

    lax.fori_loop(0, hi_ref.shape[0] // STEP_HEADS, some_heads, 0)


IN_SMEM = pl.BlockSpec(memory_space=pltpu.SMEM)
IN_VMEM = pl.BlockSpec(memory_space=pltpu.VMEM)
IN_ANY = pl.BlockSpec(memory_space=pl.ANY)


def query_features(g, groups, parts, meta, ratio, queries, query_maps):
    piece = jax.ShapeDtypeStruct((groups, queries.shape[0] * BLOCK, FAR_ROWS), bf16)
    return pl.pallas_call(
        functools.partial(feature_kernel, parts, g * groups),
        out_shape=[piece] * 2,
        in_specs=[IN_SMEM, IN_SMEM, IN_VMEM, IN_VMEM],
        out_specs=[IN_VMEM] * 2,
        compiler_params=pltpu.CompilerParams(vmem_limit_bytes=VMEM_LIMIT),
        cost_estimate=pl.CostEstimate(flops=10 ** 5, bytes_accessed=10 ** 5, transcendentals=0),
        name="query_features",
    )(meta, ratio, queries, query_maps)


def attend_kernel(
    parts, g, groups, placed,
    meta, q_ref, hi_ref, lo_ref, kmap_ref, *rest,
):
    same_layer, earlier, got_refs = rest[:4], rest[4:8], rest[8:8 + len(placed)]
    rest = rest[len(rest) - 11 - parts:]
    out_ref, *send_refs = rest[:parts]
    kv, kt, vc, vn, state, norm, norm_row, own, slots, own_sem, got_sems = rest[parts:]
    seqs = q_ref.shape[0]
    heads = STEP_HEADS
    block = meta[0]
    part = meta[1]
    rows = BLOCK // parts
    width = groups * HD
    local_width = out_ref.shape[2] // parts
    far_blocks = jnp.maximum(block - WBLK, 0)
    offsets = row_offsets(part, parts)
    row_pos = block * BLOCK + jnp.concatenate(
        [off + lax.broadcasted_iota(jnp.int32, (rows, 1), 0) for off in offsets], axis=0
    )

    def place(n):
        offset, at = placed[n]
        col = lax.rem(part + parts - offset, parts) * local_width + at * width
        there = out_ref.at[:, :, pl.ds(pl.multiple_of(col, HD), width)]
        return pltpu.make_async_copy(got_refs[n], there, got_sems.at[n])

    def place_own():
        col = part * local_width + g * width
        there = out_ref.at[:, :, pl.ds(pl.multiple_of(col, HD), width)]
        return pltpu.make_async_copy(own, there, own_sem)

    for n in range(len(placed)):
        place(n).start()

    layer = block >> 2
    for n in range(NEAR):
        corner = (block & (NEAR - 1)) ^ (((n & 1) << 1) | (n >> 1))
        kv[layer * NEAR + corner] = same_layer[n][g]

        def fetch(at, carry, ref=earlier[n], corner=corner):
            kv[at * NEAR + corner] = ref[(layer ^ at) - 1]
            return carry

        lax.fori_loop(0, layer, fetch, 0)

    most = jnp.int32(0)
    for s in range(seqs):
        start = meta[2 + s]
        bits = meta[2 + seqs + s]
        slots[s, 0] = block
        count = jnp.int32(1)
        for d in range(1, WBLK + 1):
            j = block - d
            seen = (lax.shift_right_logical(bits, d - 1) & 1) == 1
            seen = seen & (j >= 0) & (j * BLOCK + BLOCK > start)
            slots[s, count] = jnp.maximum(j, 0)
            count = count + seen.astype(jnp.int32)
        slots[s, WBLK + 2] = count
        most = jnp.maximum(most, count)
    slots[0, WBLK + 3] = most
    for i in range(PAIRS):

        @pl.when((2 * i < most) | (i < LEAST_PAIRS))
        def _():
            cols = slice(i * PAIR, (i + 1) * PAIR)
            for s in range(seqs):
                start = meta[2 + s]
                count = slots[s, WBLK + 2]
                j0 = jnp.where(2 * i < count, slots[s, 2 * i], 0)
                j1 = jnp.where(2 * i + 1 < count, slots[s, 2 * i + 1], 0)
                both = jnp.concatenate([kv[j0, s], kv[j1, s]], axis=0)
                k_hi, k_lo = split2(jnp.transpose(both[:, :HD] * (LOG2E * HD ** -0.5)))
                kt[s, 0:HD, cols] = k_hi
                kt[s, HD:2 * HD, cols] = k_hi
                kt[s, 2 * HD:3 * HD, cols] = k_lo
                v_hi, v_lo = split2(both[:, HD:])
                lines = slice(FAR_ROWS + i * PAIR, FAR_ROWS + (i + 1) * PAIR)
                vc[s, lines, 0:HD] = v_hi
                vc[s, lines, HD:2 * HD] = v_lo
                vn[s, lines, :] = jnp.concatenate([v_hi, jnp.zeros_like(v_hi)], axis=1)
                col = lax.broadcasted_iota(jnp.int32, (1, PAIR), 1)
                second = col >= BLOCK
                key_pos = jnp.where(second, j1, j0) * BLOCK + (col & (BLOCK - 1))
                slot = 2 * i + second.astype(jnp.int32)
                allowed = (slot < count) & (key_pos >= start) & (key_pos <= row_pos)
                bias = jnp.where(allowed, 0.0, NEG)
                bias = jnp.concatenate([bias, jnp.zeros_like(bias)], axis=0)
                kt[s, 3 * HD:4 * HD, cols] = bias.astype(bf16)

    state[...] = jnp.zeros_like(state)
    norm[...] = jnp.zeros_like(norm)

    @pl.when(far_blocks > 0)
    def _():
        w_hi, w_lo = split2(jnp.transpose(kmap_ref[g]))
        w_cat = jnp.concatenate([w_hi, w_hi, w_lo], axis=1)

        def far_step(c, carry):
            for s in range(seqs):
                start = meta[2 + s]
                span = jnp.concatenate([kv[c * NEAR + n, s] for n in range(NEAR)], axis=0)
                t_hi, t_lo = split2(jnp.transpose(span[:, :HD]))
                logits = mm(w_cat, jnp.concatenate([t_hi, t_lo, t_hi], axis=0))
                up = jnp.exp(logits)
                down = jnp.exp(-logits)
                pos = c * NEAR * BLOCK + lax.broadcasted_iota(jnp.int32, (1, NEAR * BLOCK), 1)
                keep = (pos >= start) & (pos < far_blocks * BLOCK)
                up_scale = jnp.where(keep, 1.0 / jnp.sum(up, axis=0, keepdims=True), 0.0)
                down_scale = jnp.where(keep, 1.0 / jnp.sum(down, axis=0, keepdims=True), 0.0)
                feats = jnp.concatenate([up * up_scale, down * down_scale], axis=0)
                p_hi, p_lo = split2(feats)
                v_hi, v_lo = split2(span[:, HD:])
                wide = mm(p_hi, jnp.concatenate([v_hi, v_lo], axis=1))
                state[s] += wide[:, :HD] + wide[:, HD:] + mm(p_lo, v_hi)
                norm[s] += jnp.broadcast_to(jnp.sum(feats, axis=1, keepdims=True), norm.shape[1:])
            return carry

        lax.fori_loop(0, (far_blocks + NEAR - 1) // NEAR, far_step, 0)

    for s in range(seqs):
        s_hi, s_lo = split2(state[s])
        vc[s, :FAR_ROWS, :] = jnp.concatenate([s_hi, s_lo], axis=1)
        vn[s, :FAR_ROWS, :] = jnp.concatenate([s_hi, norm[s].astype(bf16)], axis=1)
        norm_row[s] = jnp.transpose(norm[s])[:8]

    def attend_rows(pairs, step, carry):
        span = pairs * PAIR
        lines = FAR_ROWS + span
        pick = lax.broadcasted_iota(jnp.int32, (BLOCK, HD), 0) == lax.broadcasted_iota(
            jnp.int32, (BLOCK, HD), 1
        )
        pick = jnp.where(pick, 1.0, 0.0).astype(bf16)
        units = [
            (s, range(h, h + UNIT_HEADS)) for h in range(0, heads, UNIT_HEADS) for s in range(seqs)
        ]

        def scores_of(s, hs):
            pieces = []
            for h in hs:
                x_hi, x_lo = split2(head_rows(q_ref, s, g * groups + step * heads + h, offsets))
                pieces.append(jnp.concatenate([x_hi, x_lo, x_hi, pick], axis=1))
            return mm(jnp.concatenate(pieces, axis=0), kt[s, :, :span])

        def finish(s, hs, scores):
            terms = jnp.exp2(scores - jnp.max(scores, axis=1, keepdims=True))
            p_hi, p_lo = split2(terms)
            mine = slice(s * BLOCK, (s + 1) * BLOCK)
            f_hi = jnp.concatenate([hi_ref[step * heads + h, mine, :] for h in hs], axis=0)
            f_lo = jnp.concatenate([lo_ref[step * heads + h, mine, :] for h in hs], axis=0)
            weighed = f_hi.astype(f32) * norm_row[s, 0:1, :]
            parts_of_den = [weighed[:, :HALF], weighed[:, HALF:]]
            parts_of_den += [terms[:, n * HD:(n + 1) * HD] for n in range(span // HD)]
            den = jnp.sum(sum(parts_of_den[1:], parts_of_den[0]), axis=1, keepdims=True)
            wide = mm(jnp.concatenate([f_hi, p_hi], axis=1), vc[s, :lines, :])
            rest = mm(jnp.concatenate([f_lo, p_lo], axis=1), vn[s, :lines, :])
            den = den + rest[:, HD:]
            inverse = pl.reciprocal(den, approx=True)
            inverse = inverse * (2.0 - den * inverse)
            result = (wide[:, :HD] + wide[:, HD:] + rest[:, :HD]) * inverse
            live = row_pos >= meta[2 + s]
            for n, h in enumerate(hs):
                out = jnp.where(live, result[n * BLOCK:(n + 1) * BLOCK], 0.0)
                cols = pl.ds(pl.multiple_of((step * heads + h) * HD, HD), HD)
                for m, ref in enumerate(send_refs):
                    ref[s, :, cols] = out[m * rows:(m + 1) * rows]
                own[s, :, cols] = out[(parts - 1) * rows:]

        ahead = scores_of(*units[0])
        for n, unit in enumerate(units):
            scores = ahead
            if n + 1 < len(units):
                ahead = scores_of(*units[n + 1])
            finish(*unit, scores)
        return carry

    pairs_now = jnp.maximum((slots[0, WBLK + 3] + 1) // 2, LEAST_PAIRS)
    for pairs in range(LEAST_PAIRS, PAIRS + 1):

        @pl.when(pairs_now == pairs)
        def _():
            lax.fori_loop(0, groups // heads, functools.partial(attend_rows, pairs), 0)

    place_own().start()
    for n in range(len(placed)):
        place(n).wait()
    place_own().wait()


def attend(g, groups, parts, meta, queries, features, key_maps, gathered, out, received):
    seqs, _, local_width = queries.shape
    rows = BLOCK // parts
    width = groups * HD
    piece = jax.ShapeDtypeStruct((seqs, rows, width), f32)
    whole = jax.ShapeDtypeStruct((seqs, rows, local_width * parts), f32)
    placed = tuple(where for where, _ in received)
    extra = [value for _, value in received] + ([] if out is None else [out])
    keys = PAIRS * PAIR
    return pl.pallas_call(
        functools.partial(attend_kernel, parts, g, groups, placed),
        out_shape=[whole] + [piece] * (parts - 1),
        input_output_aliases={} if out is None else {13 + len(received): 0},
        in_specs=[IN_SMEM] + [IN_VMEM] * 12 + [IN_ANY] * len(extra),
        out_specs=[IN_ANY] + [IN_VMEM] * (parts - 1),
        scratch_shapes=[
            pltpu.VMEM((NEAR * (gathered[-1].shape[0] + 1), seqs, BLOCK, 2 * HD), f32),
            pltpu.VMEM((seqs, 4 * HD, keys), bf16),
            pltpu.VMEM((seqs, FAR_ROWS + keys, 2 * HD), bf16),
            pltpu.VMEM((seqs, FAR_ROWS + keys, 2 * HD), bf16),
            pltpu.VMEM((seqs, FAR_ROWS, HD), f32),
            pltpu.VMEM((seqs, FAR_ROWS, HD), f32),
            pltpu.VMEM((seqs, 8, FAR_ROWS), f32),
            pltpu.VMEM((seqs, rows, width), f32),
            pltpu.SMEM((seqs, WBLK + 4), jnp.int32),
            pltpu.SemaphoreType.DMA,
            pltpu.SemaphoreType.DMA((max(len(received), 1),)),
        ],
        compiler_params=pltpu.CompilerParams(vmem_limit_bytes=VMEM_LIMIT),
        cost_estimate=pl.CostEstimate(flops=10 ** 5, bytes_accessed=10 ** 5, transcendentals=0),
        name="attend",
    )(meta, queries, *features, key_maps, *gathered, *extra)


def swap(value, count, bit):
    return lax.ppermute(value, "ctx", [(n, n ^ bit) for n in range(count)])


def after(value, *earlier):
    return lax.optimization_barrier((value, earlier))[0]


def on_device(queries, keys, values, query_maps, key_maps, mix, window_blocks, starts):
    seqs, local_tokens, local_width = queries.shape
    local_kv = keys.shape[2] // HD
    groups = local_width // HD // local_kv
    count = lax.axis_size("ctx")
    parts = lax.axis_size("kv")
    part = lax.axis_index("kv")
    width = groups * HD
    ratio = jnp.exp(-mix)
    meta = jnp.concatenate(
        [
            jnp.stack([lax.axis_index("ctx"), part]).astype(jnp.int32),
            starts.astype(jnp.int32),
            window_blocks[:, 0].astype(jnp.int32),
        ]
    )
    def pair_of(keys, values, g):
        cols = slice(g * HD, (g + 1) * HD)
        return jnp.concatenate([keys[:, :, cols], values[:, :, cols]], axis=2)

    layers = count // NEAR
    pairs = [pair_of(keys, values, 0)]
    later_keys, later_values = after((keys, values), pairs[0])
    pairs += [pair_of(later_keys, later_values, g) for g in range(1, local_kv)]

    def z_swap(value, step):
        return swap(value, count, NEAR * step)

    def features_of(g, *earlier):
        ready = after(meta, *earlier)
        return query_features(g, groups, parts, ready, ratio, queries, query_maps)

    out = None
    waiting = []

    moved = {}
    features = []
    one = z_swap(pairs[0], 1)
    whole = jnp.stack(pairs)
    across = swap(whole, count, 2)
    same_layer = (whole, across, swap(whole, count, 1), swap(across, count, 1))
    if layers == 4:
        later = z_swap(after(pairs[1], one), 1)
        two = z_swap(after(pairs[0], one), 2)
        features.append(features_of(0, one))
        later_two = z_swap(after(pairs[1], two, later), 2)
        moved[0] = [one, two, z_swap(after(two, features[0]), 1)]
        features.append(features_of(1, two, later))
        straight = jnp.stack(after(moved[0], *features))
        if local_kv > 2:
            features.append(features_of(2, straight))
            others = jnp.stack(pairs[2:])
            last = z_swap(after(others, later), 1)
            before = (two, last)
            for n in range(2, local_kv):
                moved[n] = [last, z_swap(after(pairs[n], *before), 2)]
                before = (moved[n][1],)
            moved[2].append(z_swap(moved[2][1], 1))
        features += [features_of(g, later_two) for g in range(3, local_kv)]
        moved[1] = [later, later_two, z_swap(after(later_two, features[min(2, local_kv - 1)]), 1)]
    else:
        features = [features_of(g) for g in range(local_kv)]
        for g in range(local_kv):
            moved[g] = [z_swap(pairs[g], step) for step in range(1, layers)]
        straight = jnp.stack(after(moved[0], *features))

    def stacked(g, *earlier):
        pieces = after(moved[g], *earlier)
        return jnp.stack([piece if piece.ndim == 3 else piece[g - 2] for piece in pieces])

    crossed = after(swap(straight, count, 2), *features[2:3])
    earlier = (straight, crossed, swap(straight, count, 1), swap(crossed, count, 1))
    for g in range(local_kv):
        if g + 1 < local_kv:
            straight = stacked(g + 1, crossed)
            crossed = swap(straight, count, 2)
            other = swap(straight, count, 1)
        received = waiting.pop(0) if len(waiting) > 1 else []
        out, *sends = attend(
            g, groups, parts, meta, queries, features[g], key_maps, same_layer + earlier, out, received
        )
        before = sends[0]
        if g == 0:
            for n in range(3, local_kv):
                if len(moved[n]) == 2:
                    moved[n].append(z_swap(after(moved[n][1], before), 1))
        if waiting:
            sends = [after(piece, waiting[-1][0][1]) for piece in sends]
        waiting.append(
            [
                ((o, g), lax.ppermute(piece, "kv", [(n, (n + o) % parts) for n in range(parts)]))
                for o, piece in enumerate(sends, 1)
            ]
        )
        if g + 1 < local_kv:
            crossed = after(crossed, before)
            earlier = (straight, crossed, other, swap(crossed, count, 1))
    for (o, g), piece in sum(waiting, []):
        source = lax.rem(part + parts - o, parts)
        out = lax.dynamic_update_slice(out, piece, (0, 0, source * local_width + g * width))
    return out


def solution(mesh):
    placed = (
        P(None, "ctx", "kv"),
        P(None, "ctx", "kv"),
        P(None, "ctx", "kv"),
        P("kv", None, None),
        P("kv", None, None),
        P("kv"),
        P(None, "ctx"),
        P(),
    )
    return jax.shard_map(
        on_device,
        mesh=mesh,
        in_specs=placed,
        out_specs=P(None, ("ctx", "kv"), None),
        check_vma=False,
    )
```

```python
import functools

import jax
import jax.numpy as jnp
from jax import lax
from jax.experimental import pallas as pl
from jax.experimental.pallas import tpu as pltpu
from jax.sharding import PartitionSpec as P

HD = 128
HALF = 128
FAR_ROWS = 2 * HALF
BLOCK = 64
WBLK = 8
STEP_HEADS = 8
UNIT_HEADS = 4
PAIR = 2 * BLOCK
PAIRS = (WBLK + 2) // 2
LEAST_PAIRS = 2
NEAR = 4
LOG2E = 1.4426950408889634
NEG = -1e30
VMEM_LIMIT = 20 * 1024 * 1024

bf16 = jnp.bfloat16
f32 = jnp.float32


def split2(x):
    hi = x.astype(bf16)
    lo = (x - hi.astype(f32)).astype(bf16)
    return hi, lo


def mm(a, b):
    return lax.dot_general(a, b, (((1,), (0,)), ((), ())), preferred_element_type=f32)


def row_offsets(part, parts):
    rows = BLOCK // parts
    return [lax.rem(part + o, parts) * rows for o in range(1, parts)] + [part * rows]


def head_rows(q_ref, s, head, offsets):
    rows = BLOCK // len(offsets)
    cols = pl.ds(pl.multiple_of(head * HD, HD), HD)
    return jnp.concatenate([q_ref[s, pl.ds(pl.multiple_of(off, 8), rows), cols] for off in offsets], axis=0)


def feature_kernel(parts, first_head, meta, ratio, q_ref, maps_ref, hi_ref, lo_ref):
    seqs = q_ref.shape[0]
    offsets = row_offsets(meta[1], parts)

    def some_heads(i, carry):
        for n in range(STEP_HEADS):
            h = i * STEP_HEADS + n
            head = first_head + h
            x = jnp.concatenate([head_rows(q_ref, s, head, offsets) for s in range(seqs)], axis=0)
            x_hi, x_lo = split2(x)
            w_hi, w_lo = split2(maps_ref[head])
            logits = mm(
                jnp.concatenate([x_hi, x_lo, x_hi], axis=1),
                jnp.concatenate([w_hi, w_hi, w_lo], axis=0),
            )
            for m, raw in enumerate((jnp.exp(logits), jnp.exp(-logits))):
                feats = raw * (ratio[head] / jnp.sum(raw, axis=1, keepdims=True))
                p_hi, p_lo = split2(feats)
                hi_ref[h, :, m * HALF:(m + 1) * HALF] = p_hi
                lo_ref[h, :, m * HALF:(m + 1) * HALF] = p_lo
        return carry

    lax.fori_loop(0, hi_ref.shape[0] // STEP_HEADS, some_heads, 0)


IN_SMEM = pl.BlockSpec(memory_space=pltpu.SMEM)
IN_VMEM = pl.BlockSpec(memory_space=pltpu.VMEM)
IN_ANY = pl.BlockSpec(memory_space=pl.ANY)


def query_features(g, groups, parts, meta, ratio, queries, query_maps):
    piece = jax.ShapeDtypeStruct((groups, queries.shape[0] * BLOCK, FAR_ROWS), bf16)
    return pl.pallas_call(
        functools.partial(feature_kernel, parts, g * groups),
        out_shape=[piece] * 2,
        in_specs=[IN_SMEM, IN_SMEM, IN_VMEM, IN_VMEM],
        out_specs=[IN_VMEM] * 2,
        compiler_params=pltpu.CompilerParams(vmem_limit_bytes=VMEM_LIMIT),
        cost_estimate=pl.CostEstimate(flops=10 ** 5, bytes_accessed=10 ** 5, transcendentals=0),
        name="query_features",
    )(meta, ratio, queries, query_maps)


def attend_kernel(
    parts, g, groups, placed,
    meta, q_ref, hi_ref, lo_ref, kmap_ref, *rest,
):
    same_layer, earlier, got_refs = rest[:4], rest[4:8], rest[8:8 + len(placed)]
    rest = rest[len(rest) - 11 - parts:]
    out_ref, *send_refs = rest[:parts]
    kv, kt, vc, vn, state, norm, norm_row, own, slots, own_sem, got_sems = rest[parts:]
    seqs = q_ref.shape[0]
    block = meta[0]
    part = meta[1]
    rows = BLOCK // parts
    width = groups * HD
    local_width = out_ref.shape[2] // parts
    far_blocks = jnp.maximum(block - WBLK, 0)
    offsets = row_offsets(part, parts)
    row_pos = block * BLOCK + jnp.concatenate(
        [off + lax.broadcasted_iota(jnp.int32, (rows, 1), 0) for off in offsets], axis=0
    )

    def place(n):
        offset, at = placed[n]
        col = lax.rem(part + parts - offset, parts) * local_width + at * width
        there = out_ref.at[:, :, pl.ds(pl.multiple_of(col, HD), width)]
        return pltpu.make_async_copy(got_refs[n], there, got_sems.at[n])

    def place_own():
        col = part * local_width + g * width
        there = out_ref.at[:, :, pl.ds(pl.multiple_of(col, HD), width)]
        return pltpu.make_async_copy(own, there, own_sem)

    for n in range(len(placed)):
        place(n).start()

    layer = block >> 2
    for n in range(NEAR):
        corner = (block & (NEAR - 1)) ^ (((n & 1) << 1) | (n >> 1))
        kv[layer * NEAR + corner] = same_layer[n][g]

        def fetch(at, carry, ref=earlier[n], corner=corner):
            kv[at * NEAR + corner] = ref[(layer ^ at) - 1]
            return carry

        lax.fori_loop(0, layer, fetch, 0)

    most = jnp.int32(0)
    for s in range(seqs):
        start = meta[2 + s]
        bits = meta[2 + seqs + s]
        slots[s, 0] = block
        count = jnp.int32(1)
        for d in range(1, WBLK + 1):
            j = block - d
            seen = (lax.shift_right_logical(bits, d - 1) & 1) == 1
            seen = seen & (j >= 0) & (j * BLOCK + BLOCK > start)
            slots[s, count] = jnp.maximum(j, 0)
            count = count + seen.astype(jnp.int32)
        slots[s, WBLK + 2] = count
        most = jnp.maximum(most, count)
    for i in range(PAIRS):

        @pl.when((2 * i < most) | (i < LEAST_PAIRS))
        def _():
            cols = slice(i * PAIR, (i + 1) * PAIR)
            for s in range(seqs):
                start = meta[2 + s]
                count = slots[s, WBLK + 2]
                j0 = jnp.where(2 * i < count, slots[s, 2 * i], 0)
                j1 = jnp.where(2 * i + 1 < count, slots[s, 2 * i + 1], 0)
                both = jnp.concatenate([kv[j0, s], kv[j1, s]], axis=0)
                k_hi, k_lo = split2(jnp.transpose(both[:, :HD] * (LOG2E * HD ** -0.5)))
                kt[s, 0:HD, cols] = k_hi
                kt[s, HD:2 * HD, cols] = k_hi
                kt[s, 2 * HD:3 * HD, cols] = k_lo
                v_hi, v_lo = split2(both[:, HD:])
                lines = slice(FAR_ROWS + i * PAIR, FAR_ROWS + (i + 1) * PAIR)
                vc[s, lines, 0:HD] = v_hi
                vc[s, lines, HD:2 * HD] = v_lo
                vn[s, lines, :] = jnp.concatenate([v_hi, jnp.zeros_like(v_hi)], axis=1)
                col = lax.broadcasted_iota(jnp.int32, (1, PAIR), 1)
                second = col >= BLOCK
                key_pos = jnp.where(second, j1, j0) * BLOCK + (col & (BLOCK - 1))
                slot = 2 * i + second.astype(jnp.int32)
                allowed = (slot < count) & (key_pos >= start) & (key_pos <= row_pos)
                bias = jnp.where(allowed, 0.0, NEG)
                bias = jnp.concatenate([bias, jnp.zeros_like(bias)], axis=0)
                kt[s, 3 * HD:4 * HD, cols] = bias.astype(bf16)

    state[...] = jnp.zeros_like(state)
    norm[...] = jnp.zeros_like(norm)

    @pl.when(far_blocks > 0)
    def _():
        w_hi, w_lo = split2(jnp.transpose(kmap_ref[g]))
        w_cat = jnp.concatenate([w_hi, w_hi, w_lo], axis=1)

        def far_step(c, carry):
            for s in range(seqs):
                start = meta[2 + s]
                span = jnp.concatenate([kv[c * NEAR + n, s] for n in range(NEAR)], axis=0)
                t_hi, t_lo = split2(jnp.transpose(span[:, :HD]))
                logits = mm(w_cat, jnp.concatenate([t_hi, t_lo, t_hi], axis=0))
                up = jnp.exp(logits)
                down = jnp.exp(-logits)
                pos = c * NEAR * BLOCK + lax.broadcasted_iota(jnp.int32, (1, NEAR * BLOCK), 1)
                keep = (pos >= start) & (pos < far_blocks * BLOCK)
                up_scale = jnp.where(keep, 1.0 / jnp.sum(up, axis=0, keepdims=True), 0.0)
                down_scale = jnp.where(keep, 1.0 / jnp.sum(down, axis=0, keepdims=True), 0.0)
                feats = jnp.concatenate([up * up_scale, down * down_scale], axis=0)
                p_hi, p_lo = split2(feats)
                v_hi, v_lo = split2(span[:, HD:])
                wide = mm(p_hi, jnp.concatenate([v_hi, v_lo], axis=1))
                state[s] += wide[:, :HD] + wide[:, HD:] + mm(p_lo, v_hi)
                norm[s] += jnp.broadcast_to(jnp.sum(feats, axis=1, keepdims=True), norm.shape[1:])
            return carry

        lax.fori_loop(0, (far_blocks + NEAR - 1) // NEAR, far_step, 0)

    for s in range(seqs):
        s_hi, s_lo = split2(state[s])
        vc[s, :FAR_ROWS, :] = jnp.concatenate([s_hi, s_lo], axis=1)
        vn[s, :FAR_ROWS, :] = jnp.concatenate([s_hi, norm[s].astype(bf16)], axis=1)
        norm_row[s] = jnp.transpose(norm[s])[:8]

    def attend_rows(pairs, s):
        span = pairs * PAIR
        lines = FAR_ROWS + span
        pick = lax.broadcasted_iota(jnp.int32, (BLOCK, HD), 0) == lax.broadcasted_iota(
            jnp.int32, (BLOCK, HD), 1
        )
        pick = jnp.where(pick, 1.0, 0.0).astype(bf16)
        mine = pl.ds(pl.multiple_of(s * BLOCK, BLOCK), BLOCK)
        live = row_pos >= meta[2 + s]
        units = [range(h, h + UNIT_HEADS) for h in range(0, groups, UNIT_HEADS)]

        def scores_of(hs):
            pieces = []
            for h in hs:
                x_hi, x_lo = split2(head_rows(q_ref, s, g * groups + h, offsets))
                pieces.append(jnp.concatenate([x_hi, x_lo, x_hi, pick], axis=1))
            return mm(jnp.concatenate(pieces, axis=0), kt[s, :, :span])

        def finish(hs, scores):
            terms = jnp.exp2(scores - jnp.max(scores, axis=1, keepdims=True))
            p_hi, p_lo = split2(terms)
            f_hi = jnp.concatenate([hi_ref[h, mine, :] for h in hs], axis=0)
            f_lo = jnp.concatenate([lo_ref[h, mine, :] for h in hs], axis=0)
            weighed = f_hi.astype(f32) * norm_row[s, 0:1, :]
            parts_of_den = [weighed[:, :HALF], weighed[:, HALF:]]
            parts_of_den += [terms[:, n * HD:(n + 1) * HD] for n in range(span // HD)]
            den = jnp.sum(sum(parts_of_den[1:], parts_of_den[0]), axis=1, keepdims=True)
            wide = mm(jnp.concatenate([f_hi, p_hi], axis=1), vc[s, :lines, :])
            rest = mm(jnp.concatenate([f_lo, p_lo], axis=1), vn[s, :lines, :])
            den = den + rest[:, HD:]
            inverse = pl.reciprocal(den, approx=True)
            inverse = inverse * (2.0 - den * inverse)
            result = (wide[:, :HD] + wide[:, HD:] + rest[:, :HD]) * inverse
            for n, h in enumerate(hs):
                out = jnp.where(live, result[n * BLOCK:(n + 1) * BLOCK], 0.0)
                cols = slice(h * HD, (h + 1) * HD)
                for m, ref in enumerate(send_refs):
                    ref[s, :, cols] = out[m * rows:(m + 1) * rows]
                own[s, :, cols] = out[(parts - 1) * rows:]

        ahead = scores_of(units[0])
        for n, unit in enumerate(units):
            scores = ahead
            if n + 1 < len(units):
                ahead = scores_of(units[n + 1])
            finish(unit, scores)

    def one_sequence(s, carry):
        pairs_now = jnp.maximum((slots[s, WBLK + 2] + 1) // 2, LEAST_PAIRS)
        for pairs in range(LEAST_PAIRS, PAIRS + 1):
            pl.when(pairs_now == pairs)(functools.partial(attend_rows, pairs, s))
        return carry

    lax.fori_loop(0, seqs, one_sequence, 0)
    place_own().start()
    for n in range(len(placed)):
        place(n).wait()
    place_own().wait()


def attend(g, groups, parts, meta, queries, features, key_maps, gathered, out, received):
    seqs, _, local_width = queries.shape
    rows = BLOCK // parts
    width = groups * HD
    piece = jax.ShapeDtypeStruct((seqs, rows, width), f32)
    whole = jax.ShapeDtypeStruct((seqs, rows, local_width * parts), f32)
    placed = tuple(where for where, _ in received)
    extra = [value for _, value in received] + ([] if out is None else [out])
    keys = PAIRS * PAIR
    return pl.pallas_call(
        functools.partial(attend_kernel, parts, g, groups, placed),
        out_shape=[whole] + [piece] * (parts - 1),
        input_output_aliases={} if out is None else {13 + len(received): 0},
        in_specs=[IN_SMEM] + [IN_VMEM] * 12 + [IN_ANY] * len(extra),
        out_specs=[IN_ANY] + [IN_VMEM] * (parts - 1),
        scratch_shapes=[
            pltpu.VMEM((NEAR * (gathered[-1].shape[0] + 1), seqs, BLOCK, 2 * HD), f32),
            pltpu.VMEM((seqs, 4 * HD, keys), bf16),
            pltpu.VMEM((seqs, FAR_ROWS + keys, 2 * HD), bf16),
            pltpu.VMEM((seqs, FAR_ROWS + keys, 2 * HD), bf16),
            pltpu.VMEM((seqs, FAR_ROWS, HD), f32),
            pltpu.VMEM((seqs, FAR_ROWS, HD), f32),
            pltpu.VMEM((seqs, 8, FAR_ROWS), f32),
            pltpu.VMEM((seqs, rows, width), f32),
            pltpu.SMEM((seqs, WBLK + 3), jnp.int32),
            pltpu.SemaphoreType.DMA,
            pltpu.SemaphoreType.DMA((max(len(received), 1),)),
        ],
        compiler_params=pltpu.CompilerParams(vmem_limit_bytes=VMEM_LIMIT),
        cost_estimate=pl.CostEstimate(flops=10 ** 5, bytes_accessed=10 ** 5, transcendentals=0),
        name="attend",
    )(meta, queries, *features, key_maps, *gathered, *extra)


def swap(value, count, bit):
    return lax.ppermute(value, "ctx", [(n, n ^ bit) for n in range(count)])


def after(value, *earlier):
    return lax.optimization_barrier((value, earlier))[0]


def on_device(queries, keys, values, query_maps, key_maps, mix, window_blocks, starts):
    seqs, local_tokens, local_width = queries.shape
    local_kv = keys.shape[2] // HD
    groups = local_width // HD // local_kv
    count = lax.axis_size("ctx")
    parts = lax.axis_size("kv")
    part = lax.axis_index("kv")
    width = groups * HD
    ratio = jnp.exp(-mix)
    meta = jnp.concatenate(
        [
            jnp.stack([lax.axis_index("ctx"), part]).astype(jnp.int32),
            starts.astype(jnp.int32),
            window_blocks[:, 0].astype(jnp.int32),
        ]
    )
    def pair_of(keys, values, g):
        cols = slice(g * HD, (g + 1) * HD)
        return jnp.concatenate([keys[:, :, cols], values[:, :, cols]], axis=2)

    layers = count // NEAR
    pairs = [pair_of(keys, values, 0)]
    later_keys, later_values = after((keys, values), pairs[0])
    pairs += [pair_of(later_keys, later_values, g) for g in range(1, local_kv)]

    def z_swap(value, step):
        return swap(value, count, NEAR * step)

    def features_of(g, *earlier):
        ready = after(meta, *earlier)
        return query_features(g, groups, parts, ready, ratio, queries, query_maps)

    out = None
    waiting = []

    moved = {}
    features = []
    one = z_swap(pairs[0], 1)
    whole = jnp.stack(pairs)
    across = swap(whole, count, 2)
    same_layer = (whole, across, swap(whole, count, 1), swap(across, count, 1))
    if layers == 4:
        later = z_swap(after(pairs[1], one), 1)
        two = z_swap(after(pairs[0], one), 2)
        features.append(features_of(0, one))
        later_two = z_swap(after(pairs[1], two, later), 2)
        moved[0] = [one, two, z_swap(after(two, features[0]), 1)]
        features.append(features_of(1, two, later))
        straight = jnp.stack(after(moved[0], *features))
        features += [features_of(2, straight)] if local_kv > 2 else []
        moved[1] = [later, later_two, z_swap(after(later_two, features[-1]), 1)]
        if local_kv > 2:
            last = z_swap(after(jnp.stack(pairs[2:]), moved[1][2]), 1)
            before = (later_two,)
            for n in range(2, local_kv):
                moved[n] = [last, z_swap(after(pairs[n], *before), 2)]
                before = (moved[n][1], last)
            moved[2].append(z_swap(moved[2][1], 1))
        features += [features_of(g, later_two) for g in range(3, local_kv)]
    else:
        features = [features_of(g) for g in range(local_kv)]
        for g in range(local_kv):
            moved[g] = [z_swap(pairs[g], step) for step in range(1, layers)]
        straight = jnp.stack(after(moved[0], *features))

    def stacked(g, *earlier):
        pieces = after(moved[g], *earlier)
        return jnp.stack([piece if piece.ndim == 3 else piece[g - 2] for piece in pieces])

    crossed = after(swap(straight, count, 2), *features[2:3])
    earlier = (straight, crossed, swap(straight, count, 1), swap(crossed, count, 1))
    for g in range(local_kv):
        if g + 1 < local_kv:
            straight = stacked(g + 1, crossed)
            crossed = swap(straight, count, 2)
            other = swap(straight, count, 1)
        received = waiting.pop(0) if len(waiting) > 1 else []
        out, *sends = attend(
            g, groups, parts, meta, queries, features[g], key_maps, same_layer + earlier, out, received
        )
        before = sends[0]
        if g == 0:
            for n in range(3, local_kv):
                if len(moved[n]) == 2:
                    moved[n].append(z_swap(after(moved[n][1], before), 1))
        if waiting:
            sends = [after(piece, waiting[-1][0][1]) for piece in sends]
        waiting.append(
            [
                ((o, g), lax.ppermute(piece, "kv", [(n, (n + o) % parts) for n in range(parts)]))
                for o, piece in enumerate(sends, 1)
            ]
        )
        if g + 1 < local_kv:
            crossed = after(crossed, before)
            earlier = (straight, crossed, other, swap(crossed, count, 1))
    for (o, g), piece in sum(waiting, []):
        source = lax.rem(part + parts - o, parts)
        out = lax.dynamic_update_slice(out, piece, (0, 0, source * local_width + g * width))
    return out


def solution(mesh):
    placed = (
        P(None, "ctx", "kv"),
        P(None, "ctx", "kv"),
        P(None, "ctx", "kv"),
        P("kv", None, None),
        P("kv", None, None),
        P("kv"),
        P(None, "ctx"),
        P(),
    )
    return jax.shard_map(
        on_device,
        mesh=mesh,
        in_specs=placed,
        out_specs=P(None, ("ctx", "kv"), None),
        check_vma=False,
    )
```

```python
import functools

import jax
import jax.numpy as jnp
from jax import lax
from jax.experimental import pallas as pl
from jax.experimental.pallas import tpu as pltpu
from jax.sharding import PartitionSpec as P

HD = 128
HALF = 128
FAR_ROWS = 2 * HALF
BLOCK = 64
WBLK = 8
STEP_HEADS = 8
UNIT_HEADS = 4
PAIR = 2 * BLOCK
PAIRS = (WBLK + 2) // 2
LEAST_PAIRS = 2
NEAR = 4
LOG2E = 1.4426950408889634
NEG = -1e30
VMEM_LIMIT = 20 * 1024 * 1024

bf16 = jnp.bfloat16
f32 = jnp.float32


def split2(x):
    hi = x.astype(bf16)
    lo = (x - hi.astype(f32)).astype(bf16)
    return hi, lo


def mm(a, b):
    return lax.dot_general(a, b, (((1,), (0,)), ((), ())), preferred_element_type=f32)


def row_offsets(part, parts):
    rows = BLOCK // parts
    return [lax.rem(part + o, parts) * rows for o in range(1, parts)] + [part * rows]


def head_rows(q_ref, s, head, offsets):
    rows = BLOCK // len(offsets)
    cols = pl.ds(pl.multiple_of(head * HD, HD), HD)
    return jnp.concatenate([q_ref[s, pl.ds(pl.multiple_of(off, 8), rows), cols] for off in offsets], axis=0)


def feature_kernel(parts, first_head, meta, ratio, q_ref, maps_ref, hi_ref, lo_ref):
    seqs = q_ref.shape[0]
    offsets = row_offsets(meta[1], parts)

    def some_heads(i, carry):
        for n in range(STEP_HEADS):
            h = i * STEP_HEADS + n
            head = first_head + h
            x = jnp.concatenate([head_rows(q_ref, s, head, offsets) for s in range(seqs)], axis=0)
            x_hi, x_lo = split2(x)
            w_hi, w_lo = split2(maps_ref[head])
            logits = mm(
                jnp.concatenate([x_hi, x_lo, x_hi], axis=1),
                jnp.concatenate([w_hi, w_hi, w_lo], axis=0),
            )
            for m, raw in enumerate((jnp.exp(logits), jnp.exp(-logits))):
                feats = raw * (ratio[head] / jnp.sum(raw, axis=1, keepdims=True))
                p_hi, p_lo = split2(feats)
                hi_ref[h, :, m * HALF:(m + 1) * HALF] = p_hi
                lo_ref[h, :, m * HALF:(m + 1) * HALF] = p_lo
        return carry

    lax.fori_loop(0, hi_ref.shape[0] // STEP_HEADS, some_heads, 0)


IN_SMEM = pl.BlockSpec(memory_space=pltpu.SMEM)
IN_VMEM = pl.BlockSpec(memory_space=pltpu.VMEM)
IN_ANY = pl.BlockSpec(memory_space=pl.ANY)


def query_features(g, groups, parts, meta, ratio, queries, query_maps):
    piece = jax.ShapeDtypeStruct((groups, queries.shape[0] * BLOCK, FAR_ROWS), bf16)
    return pl.pallas_call(
        functools.partial(feature_kernel, parts, g * groups),
        out_shape=[piece] * 2,
        in_specs=[IN_SMEM, IN_SMEM, IN_VMEM, IN_VMEM],
        out_specs=[IN_VMEM] * 2,
        compiler_params=pltpu.CompilerParams(vmem_limit_bytes=VMEM_LIMIT),
        cost_estimate=pl.CostEstimate(flops=10 ** 5, bytes_accessed=10 ** 5, transcendentals=0),
        name="query_features",
    )(meta, ratio, queries, query_maps)


def attend_kernel(
    parts, g, groups, placed,
    meta, q_ref, hi_ref, lo_ref, kmap_ref, *rest,
):
    same_layer, earlier, got_refs = rest[:4], rest[4:8], rest[8:8 + len(placed)]
    rest = rest[len(rest) - 11 - parts:]
    out_ref, *send_refs = rest[:parts]
    kv, kt, vc, vn, state, norm, norm_row, own, slots, own_sem, got_sems = rest[parts:]
    seqs = q_ref.shape[0]
    block = meta[0]
    part = meta[1]
    rows = BLOCK // parts
    width = groups * HD
    local_width = out_ref.shape[2] // parts
    far_blocks = jnp.maximum(block - WBLK, 0)
    offsets = row_offsets(part, parts)
    row_pos = block * BLOCK + jnp.concatenate(
        [off + lax.broadcasted_iota(jnp.int32, (rows, 1), 0) for off in offsets], axis=0
    )

    def place(n):
        offset, at = placed[n]
        col = lax.rem(part + parts - offset, parts) * local_width + at * width
        there = out_ref.at[:, :, pl.ds(pl.multiple_of(col, HD), width)]
        return pltpu.make_async_copy(got_refs[n], there, got_sems.at[n])

    def place_own():
        col = part * local_width + g * width
        there = out_ref.at[:, :, pl.ds(pl.multiple_of(col, HD), width)]
        return pltpu.make_async_copy(own, there, own_sem)

    for n in range(len(placed)):
        place(n).start()

    layer = block >> 2
    for n in range(NEAR):
        corner = (block & (NEAR - 1)) ^ (((n & 1) << 1) | (n >> 1))
        kv[layer * NEAR + corner] = same_layer[n][g]

        def fetch(at, carry, ref=earlier[n], corner=corner):
            kv[at * NEAR + corner] = ref[(layer ^ at) - 1]
            return carry

        lax.fori_loop(0, layer, fetch, 0)

    most = jnp.int32(0)
    for s in range(seqs):
        start = meta[2 + s]
        bits = meta[2 + seqs + s]
        slots[s, 0] = block
        count = jnp.int32(1)
        for d in range(1, WBLK + 1):
            j = block - d
            seen = (lax.shift_right_logical(bits, d - 1) & 1) == 1
            seen = seen & (j >= 0) & (j * BLOCK + BLOCK > start)
            slots[s, count] = jnp.maximum(j, 0)
            count = count + seen.astype(jnp.int32)
        slots[s, WBLK + 2] = count
        most = jnp.maximum(most, count)
    for i in range(PAIRS):

        @pl.when((2 * i < most) | (i < LEAST_PAIRS))
        def _():
            cols = slice(i * PAIR, (i + 1) * PAIR)
            for s in range(seqs):
                start = meta[2 + s]
                count = slots[s, WBLK + 2]
                j0 = jnp.where(2 * i < count, slots[s, 2 * i], 0)
                j1 = jnp.where(2 * i + 1 < count, slots[s, 2 * i + 1], 0)
                both = jnp.concatenate([kv[j0, s], kv[j1, s]], axis=0)
                k_hi, k_lo = split2(jnp.transpose(both[:, :HD] * (LOG2E * HD ** -0.5)))
                kt[s, 0:HD, cols] = k_hi
                kt[s, HD:2 * HD, cols] = k_hi
                kt[s, 2 * HD:3 * HD, cols] = k_lo
                v_hi, v_lo = split2(both[:, HD:])
                lines = slice(FAR_ROWS + i * PAIR, FAR_ROWS + (i + 1) * PAIR)
                vc[s, lines, 0:HD] = v_hi
                vc[s, lines, HD:2 * HD] = v_lo
                vn[s, lines, :] = jnp.concatenate([v_hi, jnp.zeros_like(v_hi)], axis=1)
                col = lax.broadcasted_iota(jnp.int32, (1, PAIR), 1)
                second = col >= BLOCK
                key_pos = jnp.where(second, j1, j0) * BLOCK + (col & (BLOCK - 1))
                slot = 2 * i + second.astype(jnp.int32)
                allowed = (slot < count) & (key_pos >= start) & (key_pos <= row_pos)
                bias = jnp.where(allowed, 0.0, NEG)
                bias = jnp.concatenate([bias, jnp.zeros_like(bias)], axis=0)
                kt[s, 3 * HD:4 * HD, cols] = bias.astype(bf16)

    state[...] = jnp.zeros_like(state)
    norm[...] = jnp.zeros_like(norm)

    @pl.when(far_blocks > 0)
    def _():
        w_hi, w_lo = split2(jnp.transpose(kmap_ref[g]))
        w_cat = jnp.concatenate([w_hi, w_hi, w_lo], axis=1)

        def far_step(c, carry):
            for s in range(seqs):
                start = meta[2 + s]
                span = jnp.concatenate([kv[c * NEAR + n, s] for n in range(NEAR)], axis=0)
                t_hi, t_lo = split2(jnp.transpose(span[:, :HD]))
                logits = mm(w_cat, jnp.concatenate([t_hi, t_lo, t_hi], axis=0))
                up = jnp.exp(logits)
                down = jnp.exp(-logits)
                pos = c * NEAR * BLOCK + lax.broadcasted_iota(jnp.int32, (1, NEAR * BLOCK), 1)
                keep = (pos >= start) & (pos < far_blocks * BLOCK)
                up_scale = jnp.where(keep, 1.0 / jnp.sum(up, axis=0, keepdims=True), 0.0)
                down_scale = jnp.where(keep, 1.0 / jnp.sum(down, axis=0, keepdims=True), 0.0)
                feats = jnp.concatenate([up * up_scale, down * down_scale], axis=0)
                p_hi, p_lo = split2(feats)
                v_hi, v_lo = split2(span[:, HD:])
                wide = mm(p_hi, jnp.concatenate([v_hi, v_lo], axis=1))
                state[s] += wide[:, :HD] + wide[:, HD:] + mm(p_lo, v_hi)
                norm[s] += jnp.broadcast_to(jnp.sum(feats, axis=1, keepdims=True), norm.shape[1:])
            return carry

        lax.fori_loop(0, (far_blocks + NEAR - 1) // NEAR, far_step, 0)

    for s in range(seqs):
        s_hi, s_lo = split2(state[s])
        vc[s, :FAR_ROWS, :] = jnp.concatenate([s_hi, s_lo], axis=1)
        vn[s, :FAR_ROWS, :] = jnp.concatenate([s_hi, norm[s].astype(bf16)], axis=1)
        norm_row[s] = jnp.transpose(norm[s])[:8]

    def attend_rows(pairs, s):
        span = pairs * PAIR
        lines = FAR_ROWS + span
        pick = lax.broadcasted_iota(jnp.int32, (BLOCK, HD), 0) == lax.broadcasted_iota(
            jnp.int32, (BLOCK, HD), 1
        )
        pick = jnp.where(pick, 1.0, 0.0).astype(bf16)
        mine = pl.ds(pl.multiple_of(s * BLOCK, BLOCK), BLOCK)
        live = row_pos >= meta[2 + s]
        units = [range(h, h + UNIT_HEADS) for h in range(0, groups, UNIT_HEADS)]

        def scores_of(hs):
            pieces = []
            for h in hs:
                x_hi, x_lo = split2(head_rows(q_ref, s, g * groups + h, offsets))
                pieces.append(jnp.concatenate([x_hi, x_lo, x_hi, pick], axis=1))
            return mm(jnp.concatenate(pieces, axis=0), kt[s, :, :span])

        def finish(hs, scores):
            terms = jnp.exp2(scores - jnp.max(scores, axis=1, keepdims=True))
            p_hi, p_lo = split2(terms)
            f_hi = jnp.concatenate([hi_ref[h, mine, :] for h in hs], axis=0)
            f_lo = jnp.concatenate([lo_ref[h, mine, :] for h in hs], axis=0)
            weighed = f_hi.astype(f32) * norm_row[s, 0:1, :]
            parts_of_den = [weighed[:, :HALF], weighed[:, HALF:]]
            parts_of_den += [terms[:, n * HD:(n + 1) * HD] for n in range(span // HD)]
            den = jnp.sum(sum(parts_of_den[1:], parts_of_den[0]), axis=1, keepdims=True)
            wide = mm(jnp.concatenate([f_hi, p_hi], axis=1), vc[s, :lines, :])
            rest = mm(jnp.concatenate([f_lo, p_lo], axis=1), vn[s, :lines, :])
            den = den + rest[:, HD:]
            inverse = pl.reciprocal(den, approx=True)
            inverse = inverse * (2.0 - den * inverse)
            result = (wide[:, :HD] + wide[:, HD:] + rest[:, :HD]) * inverse
            for n, h in enumerate(hs):
                out = jnp.where(live, result[n * BLOCK:(n + 1) * BLOCK], 0.0)
                cols = slice(h * HD, (h + 1) * HD)
                for m, ref in enumerate(send_refs):
                    ref[s, :, cols] = out[m * rows:(m + 1) * rows]
                own[s, :, cols] = out[(parts - 1) * rows:]

        ahead = scores_of(units[0])
        for n, unit in enumerate(units):
            scores = ahead
            if n + 1 < len(units):
                ahead = scores_of(units[n + 1])
            finish(unit, scores)

    def one_sequence(s, carry):
        pairs_now = jnp.maximum((slots[s, WBLK + 2] + 1) // 2, LEAST_PAIRS)
        for pairs in range(LEAST_PAIRS, PAIRS + 1):
            pl.when(pairs_now == pairs)(functools.partial(attend_rows, pairs, s))
        return carry

    lax.fori_loop(0, seqs, one_sequence, 0)
    place_own().start()
    for n in range(len(placed)):
        place(n).wait()
    place_own().wait()


def attend(g, groups, parts, meta, queries, features, key_maps, gathered, out, received):
    seqs, _, local_width = queries.shape
    rows = BLOCK // parts
    width = groups * HD
    piece = jax.ShapeDtypeStruct((seqs, rows, width), f32)
    whole = jax.ShapeDtypeStruct((seqs, rows, local_width * parts), f32)
    placed = tuple(where for where, _ in received)
    extra = [value for _, value in received] + ([] if out is None else [out])
    keys = PAIRS * PAIR
    return pl.pallas_call(
        functools.partial(attend_kernel, parts, g, groups, placed),
        out_shape=[whole] + [piece] * (parts - 1),
        input_output_aliases={} if out is None else {13 + len(received): 0},
        in_specs=[IN_SMEM] + [IN_VMEM] * 12 + [IN_ANY] * len(extra),
        out_specs=[IN_ANY] + [IN_VMEM] * (parts - 1),
        scratch_shapes=[
            pltpu.VMEM((NEAR * (gathered[-1].shape[0] + 1), seqs, BLOCK, 2 * HD), f32),
            pltpu.VMEM((seqs, 4 * HD, keys), bf16),
            pltpu.VMEM((seqs, FAR_ROWS + keys, 2 * HD), bf16),
            pltpu.VMEM((seqs, FAR_ROWS + keys, 2 * HD), bf16),
            pltpu.VMEM((seqs, FAR_ROWS, HD), f32),
            pltpu.VMEM((seqs, FAR_ROWS, HD), f32),
            pltpu.VMEM((seqs, 8, FAR_ROWS), f32),
            pltpu.VMEM((seqs, rows, width), f32),
            pltpu.SMEM((seqs, WBLK + 3), jnp.int32),
            pltpu.SemaphoreType.DMA,
            pltpu.SemaphoreType.DMA((max(len(received), 1),)),
        ],
        compiler_params=pltpu.CompilerParams(vmem_limit_bytes=VMEM_LIMIT),
        cost_estimate=pl.CostEstimate(flops=10 ** 5, bytes_accessed=10 ** 5, transcendentals=0),
        name="attend",
    )(meta, queries, *features, key_maps, *gathered, *extra)


def swap(value, count, bit):
    return lax.ppermute(value, "ctx", [(n, n ^ bit) for n in range(count)])


def after(value, *earlier):
    return lax.optimization_barrier((value, earlier))[0]


def on_device(queries, keys, values, query_maps, key_maps, mix, window_blocks, starts):
    seqs, local_tokens, local_width = queries.shape
    local_kv = keys.shape[2] // HD
    groups = local_width // HD // local_kv
    count = lax.axis_size("ctx")
    parts = lax.axis_size("kv")
    part = lax.axis_index("kv")
    width = groups * HD
    ratio = jnp.exp(-mix)
    meta = jnp.concatenate(
        [
            jnp.stack([lax.axis_index("ctx"), part]).astype(jnp.int32),
            starts.astype(jnp.int32),
            window_blocks[:, 0].astype(jnp.int32),
        ]
    )
    def pair_of(keys, values, g):
        cols = slice(g * HD, (g + 1) * HD)
        return jnp.concatenate([keys[:, :, cols], values[:, :, cols]], axis=2)

    layers = count // NEAR
    pairs = [pair_of(keys, values, 0)]
    later_keys, later_values = after((keys, values), pairs[0])
    pairs += [pair_of(later_keys, later_values, g) for g in range(1, local_kv)]

    def z_swap(value, step):
        return swap(value, count, NEAR * step)

    def features_of(g, *earlier):
        ready = after(meta, *earlier)
        return query_features(g, groups, parts, ready, ratio, queries, query_maps)

    out = None
    waiting = []

    moved = {}
    features = []
    one = z_swap(pairs[0], 1)
    whole = jnp.stack(pairs)
    across = swap(whole, count, 2)
    same_layer = (whole, across, swap(whole, count, 1), swap(across, count, 1))
    if layers == 4:
        later = z_swap(after(pairs[1], one), 1)
        two = z_swap(after(pairs[0], one), 2)
        features.append(features_of(0, one))
        later_two = z_swap(after(pairs[1], two, later), 2)
        moved[0] = [one, two, z_swap(after(two, features[0]), 1)]
        features.append(features_of(1, two, later))
        straight = jnp.stack(after(moved[0], *features))
        features += [features_of(2, straight)] if local_kv > 2 else []
        moved[1] = [later, later_two, z_swap(after(later_two, features[-1]), 1)]
        if local_kv > 2:
            moved[2] = [None, z_swap(after(pairs[2], later_two), 2)]
            moved[2].append(z_swap(moved[2][1], 1))
        features += [features_of(g, later_two) for g in range(3, local_kv)]
    else:
        features = [features_of(g) for g in range(local_kv)]
        for g in range(local_kv):
            moved[g] = [z_swap(pairs[g], step) for step in range(1, layers)]
        straight = jnp.stack(after(moved[0], *features))

    def stacked(g, *earlier):
        pieces = after(moved[g], *earlier)
        return jnp.stack([piece if piece.ndim == 3 else piece[g - 2] for piece in pieces])

    crossed = after(swap(straight, count, 2), *features[2:3])
    earlier = (straight, crossed, swap(straight, count, 1), swap(crossed, count, 1))
    for g in range(local_kv):
        if g + 1 < local_kv:
            straight = stacked(g + 1, crossed)
            crossed = swap(straight, count, 2)
            other = swap(straight, count, 1)
        received = waiting.pop(0) if len(waiting) > 1 else []
        out, *sends = attend(
            g, groups, parts, meta, queries, features[g], key_maps, same_layer + earlier, out, received
        )
        before = sends[0]
        if g == 0 and layers == 4 and local_kv > 2:
            last = z_swap(after(jnp.stack(pairs[2:]), before), 1)
            moved[2][0] = last
            for n in range(3, local_kv):
                two = z_swap(after(pairs[n], moved[n - 1][1], last), 2)
                moved[n] = [last, two, z_swap(two, 1)]
        if waiting:
            sends = [after(piece, waiting[-1][0][1]) for piece in sends]
        waiting.append(
            [
                ((o, g), lax.ppermute(piece, "kv", [(n, (n + o) % parts) for n in range(parts)]))
                for o, piece in enumerate(sends, 1)
            ]
        )
        if g + 1 < local_kv:
            crossed = after(crossed, before)
            earlier = (straight, crossed, other, swap(crossed, count, 1))
    for (o, g), piece in sum(waiting, []):
        source = lax.rem(part + parts - o, parts)
        out = lax.dynamic_update_slice(out, piece, (0, 0, source * local_width + g * width))
    return out


def solution(mesh):
    placed = (
        P(None, "ctx", "kv"),
        P(None, "ctx", "kv"),
        P(None, "ctx", "kv"),
        P("kv", None, None),
        P("kv", None, None),
        P("kv"),
        P(None, "ctx"),
        P(),
    )
    return jax.shard_map(
        on_device,
        mesh=mesh,
        in_specs=placed,
        out_specs=P(None, ("ctx", "kv"), None),
        check_vma=False,
    )
```
